128 devices in a mesh: replica: 4 (over z_hi, core), expert: 8 (over y, z_lo), tensor: 4 (over x).
Axes of the slice: x: 4, y: 4, z: 4 (z_hi: 2, z_lo: 2; z = z_hi * 2 + z_lo), core: 2. Of those that a mesh axis runs over, the one named last changes fastest.
Arguments:
- states: bfloat16 [512, 4096], P(('replica', 'expert'), 'tensor'), may hold values from -6 to 6
- gain: float32 [4096], replicated, may hold values from 0.1 to 1.9
- route_ids: int32 [3, 512, 4], P(None, ('replica', 'expert')), may hold values from 0 to 15, all different within a row; in each aligned block of 16 rows (0 to 15, 16 to 31, ..., all dimensions but the last counted through in order) at most 8 rows name the same one
- route_weights: float32 [3, 512, 4], P(None, ('replica', 'expert')), may hold values from 0.1 to 1
- gate_w: bfloat16 [16, 4096, 1536], P('expert', None, 'tensor'), may hold values from -0.09375 to 0.09375
- up_w: bfloat16 [16, 4096, 1536], P('expert', None, 'tensor'), may hold values from -0.09375 to 0.09375
- down_w: bfloat16 [16, 1536, 4096], P('expert', 'tensor'), may hold values from -0.15625 to 0.15625
- gate_a: bfloat16 [16, 32, 4096], P('expert', 'replica'), may hold values from -0.09375 to 0.09375
- gate_b: bfloat16 [16, 32, 1536], P('expert', 'replica', 'tensor'), may hold values from -0.5 to 0.5
- up_a: bfloat16 [16, 32, 4096], P('expert', 'replica'), may hold values from -0.09375 to 0.09375
- up_b: bfloat16 [16, 32, 1536], P('expert', 'replica', 'tensor'), may hold values from -0.5 to 0.5
- down_a: bfloat16 [16, 32, 1536], P('expert', 'replica', 'tensor'), may hold values from -0.15625 to 0.15625
- down_b: bfloat16 [16, 32, 4096], P('expert', 'replica'), may hold values from -0.8984375 to 0.8984375
Outputs:
- new_states: float32 [512, 4096], P(('replica', 'expert'), 'tensor')
- last_update: float32 [512, 4096], P(('replica', 'expert'), 'tensor')
The draws below stay inside these ranges and needn't reach their ends.
Inputs may be any that keep to these rules, and one draw needn't show every extreme that they name: `route_ids`: each row names 4 different experts. In each step, the 16 rows of one device (aligned blocks of rows) name no expert more than 8 times, and in some blocks one expert exactly 8 times.
All inputs are finite; a program needn't handle non-finite values.
Results may differ from the reference program's by a relative error of at most 0.02.
Values may be sent and summed in bfloat16 or wider, within the bound.
A program may use at most 128 MiB of HBM per device.

```python
import math
import jax
import jax.numpy as jnp
import numpy as np
from jax import lax

D = 4096
FF = 1536
RANK = 32
EXPERTS = 16
TOP = 4
STEPS = 3
ROW_DEV = 16
CAP = 8
ROWS = 512


def shard_levels(rng, extent, cuts, least, high):
    def one(dim, shards_of):
        draws = jax.random.uniform(jax.random.fold_in(jax.random.fold_in(rng, 6), dim), (shards_of,), jnp.float32, least / len(cuts), high / len(cuts))
        return jnp.repeat(jnp.exp(draws), extent[dim] // shards_of).reshape((-1,) + (1,) * (len(extent) - dim - 1))

    factor_of = one(*cuts[0])
    for cut in cuts[1:]:
        factor_of = factor_of * one(*cut)
    return factor_of


def routed_block(key, own, number, rows, amount, top, bound, lean):
    sequence = jax.random.permutation(key, amount)
    crowded, usual = portions_of(amount, rows * top, bound, lean, True), portions_of(amount, rows * top, bound, lean, False)
    places = jnp.arange(amount)

    def named(tallies, offset_by):
        used = int((tallies > 0).sum())
        fixed = max(1, used // 4)
        passed = fixed + (places - fixed + offset_by * (used - fixed)) % max(1, amount - fixed)
        return jnp.zeros((amount,), jnp.int32).at[sequence[jnp.where(places < fixed, places, passed)]].set(jnp.asarray(tallies, jnp.int32))

    tallies = jnp.where(number % 4 == 0, named(crowded, number // 4), named(usual, number - number // 4 - 1))
    mixed = jax.random.permutation(jax.random.fold_in(own, 3), amount)
    giver, taker = mixed[0:amount // 2 * 2:2], mixed[1:amount // 2 * 2:2]
    room = jnp.minimum(tallies[giver] - 1, bound - tallies[taker]) // 2
    room = jnp.where((giver == sequence[0]) | (taker == sequence[0]) | (tallies[taker] == 0), 0, jnp.maximum(room, 0))
    passed = jax.random.randint(jax.random.fold_in(own, 4), (amount // 2,), 0, 1 << 20) % (room + 1)
    tallies = tallies.at[giver].add(-passed).at[taker].add(passed)
    labels = jnp.searchsorted(jnp.cumsum(tallies), jnp.arange(rows * top), side="right").astype(jnp.int32)
    listing = labels.reshape(top, rows).T
    listing = listing[jax.random.permutation(jax.random.fold_in(own, 1), rows)]
    offset_by = jax.random.randint(jax.random.fold_in(own, 2), (rows, 1), 0, top)
    return jnp.take_along_axis(listing, (jnp.arange(top)[None, :] + offset_by) % top, axis=1)


def portions_of(number_of, total, limit, slope, full):
    weights = [(1 << 20) // math.isqrt(rank ** slope) + 1 for rank in range(1, number_of + 1)]
    largest = limit if full else min(limit, max(-(-total // number_of), total * weights[0] // sum(weights)))
    least = 1 if total - largest >= number_of - 1 else 0
    holding, spare = [largest] + [least] * (number_of - 1), total - largest - least * (number_of - 1)
    while spare > 0:
        candidates = [i for i in range(1, number_of) if holding[i] < largest] or [i for i in range(1, number_of) if holding[i] < limit]
        whole, budget = sum([weights[i] for i in candidates]), spare
        for i in candidates:
            extra = min(limit - holding[i], max(1, budget * weights[i] // whole), spare)
            holding[i] = holding[i] + extra
            spare = spare - extra
    return np.array(holding)


def scatter_about(own_key, shape, scale, bound, split=(), kind=jnp.bfloat16):
    array = scale * jax.random.normal(own_key, shape, jnp.float32)
    if split:
        array = array * shard_levels(own_key, shape, split, -0.22, 0.18)
    return jnp.clip(array, -bound, bound).astype(kind)


def setup_inputs(seed: int = 0) -> dict:
    keys = jax.random.split(jax.random.key(seed), 14)
    states = scatter_about(keys[0], (ROWS, D), 1.0, 6.0, ((0, 32), (1, 4)))
    gain = jnp.clip(1.0 + 0.18 * jax.random.normal(keys[1], (D,), jnp.float32), 0.1, 1.9)
    route_ids_keys = jax.random.split(jax.random.fold_in(keys[2], 1), STEPS * ROWS // ROW_DEV)
    route_ids_turns = jax.random.permutation(jax.random.fold_in(keys[2], 3), STEPS * ROWS // ROW_DEV)
    route_ids = jax.vmap(lambda own, number: routed_block(jax.random.fold_in(keys[2], 2), own, number, ROW_DEV, EXPERTS, TOP, CAP, 1))(route_ids_keys, route_ids_turns).reshape((STEPS, ROWS, TOP))
    route_weights = jnp.clip(jnp.exp(math.log(1.0) - 2.3025851 * jax.random.uniform(keys[3], (STEPS, ROWS, TOP), jnp.float32) ** shard_levels(keys[3], (STEPS, ROWS, TOP), ((1, 32),), -0.2, 0.2)), 0.1, 1.0)
    gate_w = scatter_about(keys[4], (EXPERTS, D, FF), D ** -0.5, 0.09375, ((0, 8), (2, 4)))
    up_w = scatter_about(keys[5], (EXPERTS, D, FF), D ** -0.5, 0.09375, ((0, 8), (2, 4)))
    down_w = scatter_about(keys[6], (EXPERTS, FF, D), FF ** -0.5, 0.15625, ((0, 8), (1, 4)))
    gate_a = scatter_about(keys[7], (EXPERTS, RANK, D), D ** -0.5, 0.09375, ((0, 8), (1, 4)))
    gate_b = scatter_about(keys[8], (EXPERTS, RANK, FF), 0.08, 0.5, ((0, 8), (1, 4), (2, 4)))
    up_a = scatter_about(keys[9], (EXPERTS, RANK, D), D ** -0.5, 0.09375, ((0, 8), (1, 4)))
    up_b = scatter_about(keys[10], (EXPERTS, RANK, FF), 0.08, 0.5, ((0, 8), (1, 4), (2, 4)))
    down_a = scatter_about(keys[11], (EXPERTS, RANK, FF), FF ** -0.5, 0.15625, ((0, 8), (1, 4), (2, 4)))
    down_b = scatter_about(keys[12], (EXPERTS, RANK, D), 0.15, 0.8984375, ((0, 8), (1, 4)))
    return {"states": states, "gain": gain, "route_ids": route_ids, "route_weights": route_weights, "gate_w": gate_w, "up_w": up_w, "down_w": down_w, "gate_a": gate_a, "gate_b": gate_b, "up_a": up_a, "up_b": up_b, "down_a": down_a, "down_b": down_b}


EPS = 1e-06

def normalize(rows, gain):
    wide = rows.astype(jnp.float32)
    mean_square = lax.optimization_barrier(jnp.mean(wide * wide, axis=-1, keepdims=True))
    return (wide * lax.rsqrt(mean_square + EPS) * gain).astype(jnp.bfloat16)

def merge_weight(base, left, right):
    delta = jnp.dot(left.T, right, preferred_element_type=jnp.float32)
    return (base.astype(jnp.float32) + 2.0 * delta).astype(jnp.bfloat16)

def reference(states, gain, route_ids, route_weights, gate_w, up_w, down_w, gate_a, gate_b, up_a, up_b, down_a, down_b):

    def merge_expert(pieces):
        base_gate, base_up, base_down, gate_left, gate_right, up_left, up_right, down_left, down_right = pieces
        return (merge_weight(base_gate, gate_left, gate_right), merge_weight(base_up, up_left, up_right), merge_weight(base_down, down_left, down_right))
    merged_gate, merged_up, merged_down = lax.map(merge_expert, (gate_w, up_w, down_w, gate_a, gate_b, up_a, up_b, down_a, down_b))
    blocks = ROWS // ROW_DEV
    width = ROW_DEV * TOP
    block_index = jnp.broadcast_to(jnp.arange(blocks, dtype=jnp.int32)[:, None], (blocks, width))
    row_index = block_index * ROW_DEV + (jnp.arange(width, dtype=jnp.int32) // TOP)[None, :]
    experts_iota = jnp.arange(EXPERTS, dtype=jnp.int32)
    current = states.astype(jnp.float32)
    update = jnp.zeros((ROWS, D), jnp.float32)
    for step in range(STEPS):
        normed = normalize(current, gain)
        chosen = route_ids[step].reshape(blocks, width).astype(jnp.int32)
        onehot = (chosen[:, :, None] == experts_iota[None, None, :]).astype(jnp.int32)
        prior = jnp.cumsum(onehot, axis=1) - onehot
        slots = lax.optimization_barrier(jnp.sum(prior * onehot, axis=2)).astype(jnp.int32)
        slot_table = jnp.full((EXPERTS, blocks, CAP), ROWS, jnp.int32).at[chosen, block_index, slots].set(row_index)
        padded_rows = jnp.concatenate([normed, jnp.zeros((1, D), jnp.bfloat16)], axis=0)

        def run_expert(pieces):
            table_rows, gate_matrix, up_matrix, down_matrix = pieces
            taken = padded_rows[table_rows.reshape(-1)]
            gate = jnp.dot(taken, gate_matrix, preferred_element_type=jnp.float32)
            upper = jnp.dot(taken, up_matrix, preferred_element_type=jnp.float32)
            hidden = (jax.nn.silu(gate) * upper).astype(jnp.bfloat16)
            return jnp.dot(hidden, down_matrix, preferred_element_type=jnp.float32).astype(jnp.bfloat16)
        outputs = lax.map(run_expert, (slot_table, merged_gate, merged_up, merged_down))
        outputs = outputs.reshape(EXPERTS, blocks, CAP, D)
        picked = outputs[chosen, block_index, slots].astype(jnp.float32).reshape(ROWS, TOP, D)
        raw = route_weights[step]
        mixing = raw / lax.optimization_barrier(jnp.sum(raw, axis=-1, keepdims=True))
        update = lax.optimization_barrier(jnp.sum(picked * mixing[:, :, None], axis=1))
        current = current + update
    return (current, update)
```

```python
import jax
import jax.numpy as jnp
from jax import lax
from jax.experimental import pallas as pl
from jax.experimental.pallas import tpu as pltpu
from jax.sharding import PartitionSpec as P

EPS = 1e-06
MESH = pl.DeviceIdType.MESH
BF = jnp.bfloat16
F32 = jnp.float32
NT = (((1,), (1,)), ((), ()))
ORDER = (2, 1, 3, 0)


def kernel(
    states, gain, ids, weights, ga, gb, ua, ub, da, db, gw, uw, dw,
    out_state, out_update,
    w, wd, abuf, sbuf, bd, adt, mixb, mixs, cur, upd, gs, gi, xb, acc, uacc, ssq, hbuf, vbuf, po, rb, s2, r2,
    wsem, ad_s, ad_r, mx_s, mx_r, a1s, a1r, a2s, a2r, b1s, b1r, b2s, b2r,
):
    r, e, t = lax.axis_index("replica"), lax.axis_index("expert"), lax.axis_index("tensor")
    y, z = e // 2, e % 2
    core = r % 2
    half = r // 2
    far = r + 2 - 4 * half
    other = r + 1 - 2 * core
    across = r + core * (2 - 4 * half)

    def dev(dt=0, dy=0, dz=0):
        return (across if dz else r, (y + dy) % 4 * 2 + (1 - z if dz else z), (t + dt) % 4)

    def peer(h, d, dz=0):
        return dev(dt=d, dz=dz) if h == 0 else dev(dy=d, dz=dz)

    def remote(src, dst, ss, rs, to):
        return pltpu.make_async_remote_copy(
            src_ref=src, dst_ref=dst, send_sem=ss, recv_sem=rs, device_id=to, device_id_type=MESH
        )

    loads = []
    for j in range(2):
        for m, ref in enumerate((gw, uw)):
            loads.append((ref.at[j], w.at[:, pl.ds(j * 768 + m * 384, 384)]))
    for j in range(2):
        loads.append((dw.at[j], wd.at[pl.ds(j * 384, 384)]))
    loads = [pltpu.make_async_copy(a, b, wsem.at[i]) for i, (a, b) in enumerate(loads)]
    for copy in loads:
        copy.start()

    plane = [(d, dz) for d in range(4) for dz in range(2) if (d, dz) != (0, 0)]
    everyone = [peer(0, d, dz) for d, dz in plane] + [peer(1, d, dz) for d, dz in plane if d]
    everyone += [(far, e, t), (other, e, t)]
    barrier = pltpu.get_barrier_semaphore()
    for to in everyone:
        pl.semaphore_signal(barrier, inc=1, device_id=to, device_id_type=MESH)

    cur[...] = states[...].astype(F32)
    for c in range(8):
        row = jnp.concatenate([gain[pl.ds(4 * c + i, 1), :] for i in range(4)], axis=1)
        gs[c] = row
        gi[c] = 1.0 / row
    lane = lax.broadcasted_iota(jnp.int32, (16, 128), 1)
    mix = jnp.zeros((16, 128), F32)
    for s in range(3):
        raw = weights[s]
        raw = raw / jnp.sum(raw, axis=1, keepdims=True)
        chosen = ids[s]
        for k in range(4):
            mix = mix + jnp.where(lane == chosen[:, k : k + 1] + 16 * s, raw[:, k : k + 1], 0.0)
    mixb[y, z] = mix

    def pack(ref, scale):
        return (jnp.concatenate([ref[0].astype(F32), ref[1].astype(F32)], axis=0) * scale).astype(BF)

    abuf[r, 0] = pack(ga, 1.0)
    abuf[r, 1] = pack(ua, 1.0)
    sbuf[r, 0] = pack(gb, 2.0)
    sbuf[r, 1] = pack(ub, 2.0)
    sbuf[r, 2] = pack(da, 1.0)
    wd[pl.ds(pl.multiple_of(768 + 16 * r, 16), 16), :] = pack(db, 2.0)

    pl.semaphore_wait(barrier, len(everyone))

    def ranks(q, kind, to):
        rows = wd.at[pl.ds(pl.multiple_of(768 + 16 * q, 16), 16)]
        refs = (abuf.at[q], sbuf.at[q], rows)
        return [remote(x, x, ad_s.at[kind, i], ad_r.at[kind, i], to) for i, x in enumerate(refs)]

    to_far = ranks(r, 0, (far, e, t))
    to_other = ranks(r, 1, (other, e, t))
    passed_on = ranks(far, 2, (other, e, t))
    mixes = [
        remote(mixb.at[y, z], mixb.at[y, z], mx_s.at[2 * d + dz], mx_r.at[2 * d + dz], peer(1, d, dz)) for d, dz in plane
    ]

    def step(s, carry):
        for h in range(2):
            cols = slice(h * 512, h * 512 + 512)
            xb[h, t, y, z] = (cur[:, cols] * gs[2 * t + h]).astype(BF)
        first = {}
        for d, dz in sorted(plane, key=lambda p: -p[1]):
            for h in range(2):
                block = xb.at[h, t, y, z]
                i = 2 * d + dz
                first[h, d, dz] = remote(block, block, a1s.at[h, i], a1r.at[h, i], peer(h, d, dz))
                first[h, d, dz].start()

        @pl.when(s == 0)
        def _():
            for copy in mixes + to_far + to_other:
                copy.start()

        second = {}
        for d in range(4):
            for h in range(2):
                for dz in range(2):
                    if (d, dz) != (0, 0):
                        first[h, d, dz].wait_recv()
                block = xb.at[0, (t - d + 4) % 4, y] if h == 0 else xb.at[1, t, (y - d + 4) % 4]
                for p in ORDER[:3]:
                    second[h, d, p] = remote(block, block, a2s.at[h, d, p], a2r.at[h, d, p], peer(1 - h, p))
                    second[h, d, p].start()

        @pl.when(s == 0)
        def _():
            for copy in loads:
                copy.wait()

        acc[...] = jnp.zeros_like(acc)
        ssq[...] = jnp.zeros_like(ssq)

        def chunk(h, tc):
            x = xb[h, tc].reshape(128, 512)
            k0 = pl.multiple_of(tc * 1024 + h * 512, 512)
            for n in range(3):
                cols = slice(n * 512, n * 512 + 512)
                acc[:, cols] += jnp.dot(x, w[pl.ds(k0, 512), cols], preferred_element_type=F32)
            plain = x.astype(F32) * gi[2 * tc + h]
            plain = plain * plain
            ssq[...] += plain[:, :128] + plain[:, 128:256] + plain[:, 256:384] + plain[:, 384:]

        chunk(1, t)
        for d in range(4):
            for p in range(1, 4):
                second[0, d, p].wait_recv()
            chunk(0, (t - d + 4) % 4)
        for p in ORDER[:3]:
            for d in range(4):
                second[1, d, p].wait_recv()
            chunk(1, (t - p + 4) % 4)

        @pl.when(s == 0)
        def _():
            for copy in to_far:
                copy.wait_recv()
            for copy in passed_on:
                copy.start()
            for copy in to_other + passed_on + mixes:
                copy.wait_recv()
            bd[...] = jnp.zeros_like(bd)
            for q in range(4):
                for j in range(2):
                    keep = lax.broadcasted_iota(jnp.int32, (16, 384), 0) // 8 == j
                    for m in range(2):
                        part = jnp.where(keep, sbuf[q, m].astype(F32), 0.0).astype(BF)
                        bd[q * 32 + m * 16 : q * 32 + m * 16 + 16, j * 768 + m * 384 : j * 768 + m * 384 + 384] = part
                    part = jnp.where(keep, sbuf[q, 2].astype(F32), 0.0).astype(BF)
                    adt[q * 16 : q * 16 + 16, j * 384 : j * 384 + 384] = part
            for copy in to_far + to_other + passed_on + mixes:
                copy.wait_send()

        uacc[...] = jnp.zeros_like(uacc)
        for tc in range(4):
            for h in range(2):
                k0 = tc * 1024 + h * 512
                a = abuf[:, :, :, k0 : k0 + 512].reshape(128, 512)
                uacc[...] += lax.dot_general(xb[h, tc].reshape(128, 512), a, NT, preferred_element_type=F32)
        low = uacc[...].astype(BF)
        scale = lax.rsqrt(jnp.sum(ssq[...], axis=1, keepdims=True) * (1.0 / 4096.0) + EPS)
        mixed = mixb[...].reshape(128, 128)
        lanes = lax.broadcasted_iota(jnp.int32, (128, 128), 1)
        for j in range(2):
            here = jnp.sum(jnp.where(lanes == s * 16 + 2 * e + j, mixed, 0.0), axis=1, keepdims=True)
            for n in range(3):
                g0 = j * 768 + n * 128
                u0 = g0 + 384
                gate = acc[:, g0 : g0 + 128] + jnp.dot(low, bd[:, g0 : g0 + 128], preferred_element_type=F32)
                upper = acc[:, u0 : u0 + 128] + jnp.dot(low, bd[:, u0 : u0 + 128], preferred_element_type=F32)
                gate, upper = gate * scale, upper * scale
                hidden = gate / (1.0 + jnp.exp(-gate)) * upper * here
                hbuf[:, j * 384 + n * 128 : j * 384 + n * 128 + 128] = hidden.astype(BF)
        vbuf[...] = lax.dot_general(hbuf[...], adt[...], NT, preferred_element_type=F32).astype(BF)

        third = {}
        for d in ORDER:
            tc = (t + d) % 4
            for h in (1, 0):
                k0 = pl.multiple_of(tc * 1024 + h * 512, 512)
                part = jnp.dot(hbuf[...], wd[0:768, pl.ds(k0, 512)], preferred_element_type=F32)
                part = part + jnp.dot(vbuf[...], wd[768:832, pl.ds(k0, 512)], preferred_element_type=F32)
                po[h, tc] = part.astype(BF).reshape(4, 2, 16, 512)
                if h == 0:
                    for p in ORDER[:3]:
                        third[0, d, p] = remote(
                            po.at[0, tc, (y + p) % 4], rb.at[0, p - 1, tc], b1s.at[0, d, p], b1r.at[0, d, p], peer(1, p)
                        )
                        third[0, d, p].start()
                elif d:
                    for i in ORDER:
                        ys = (y + i) % 4
                        third[1, i, d] = remote(
                            po.at[1, tc, ys], rb.at[1, d - 1, ys], b1s.at[1, i, d], b1r.at[1, i, d], peer(0, d)
                        )
                        third[1, i, d].start()
        for copy in list(first.values()) + list(second.values()):
            copy.wait_send()
        fourth = {}
        for d in ORDER:
            for h in range(2):
                for p in ORDER[:3]:
                    third[h, d, p].wait_recv()
                i = (t + d) % 4 if h == 0 else (y + d) % 4
                for dz in range(2):
                    zz = 1 - z if dz else z
                    own = po[0, i, y, zz] if h == 0 else po[1, t, i, zz]
                    total = own.astype(F32)
                    for p in range(3):
                        total = total + rb[h, p, i, zz].astype(F32)
                    if (d, dz) == (0, 0):
                        upd[:, h * 512 : h * 512 + 512] = total
                    else:
                        n = 2 * d + dz
                        s2[h, n] = total.astype(BF)
                        fourth[h, d, dz] = remote(s2.at[h, n], r2.at[h, n], b2s.at[h, n], b2r.at[h, n], peer(h, d, dz))
                        fourth[h, d, dz].start()
        for copy in third.values():
            copy.wait_send()
        for h in range(2):
            cols = slice(h * 512, h * 512 + 512)
            total = upd[:, cols]
            for d, dz in plane:
                fourth[h, d, dz].wait_recv()
                total = total + r2[h, 2 * d + dz].astype(F32)
            upd[:, cols] = total
            cur[:, cols] += total
        for copy in fourth.values():
            copy.wait_send()
        return carry

    lax.fori_loop(0, 3, step, 0)
    out_state[...] = cur[...]
    out_update[...] = upd[...]


def per_device(states, gain, ids, weights, gw, uw, dw, ga, gb, ua, ub, da, db):
    vmem = pl.BlockSpec(memory_space=pltpu.VMEM)
    hbm = pl.BlockSpec(memory_space=pl.ANY)
    dma = pltpu.SemaphoreType.DMA
    scratch = [
        pltpu.VMEM((4096, 1536), BF),
        pltpu.VMEM((832, 4096), BF),
        pltpu.VMEM((4, 2, 16, 4096), BF),
        pltpu.VMEM((4, 3, 16, 384), BF),
        pltpu.VMEM((128, 1536), BF),
        pltpu.VMEM((64, 768), BF),
        pltpu.VMEM((4, 2, 16, 128), F32),
        pltpu.VMEM((8, 128), F32),
        pltpu.VMEM((16, 1024), F32),
        pltpu.VMEM((16, 1024), F32),
        pltpu.VMEM((8, 1, 512), F32),
        pltpu.VMEM((8, 1, 512), F32),
        pltpu.VMEM((2, 4, 4, 2, 16, 512), BF),
        pltpu.VMEM((128, 1536), F32),
        pltpu.VMEM((128, 128), F32),
        pltpu.VMEM((128, 128), F32),
        pltpu.VMEM((128, 768), BF),
        pltpu.VMEM((128, 64), BF),
        pltpu.VMEM((2, 4, 4, 2, 16, 512), BF),
        pltpu.VMEM((2, 3, 4, 2, 16, 512), BF),
        pltpu.VMEM((2, 8, 16, 512), BF),
        pltpu.VMEM((2, 8, 16, 512), BF),
        dma((6,)),
        dma((3, 3)),
        dma((3, 3)),
        dma((8,)),
        dma((8,)),
        dma((2, 8)),
        dma((2, 8)),
        dma((2, 4, 4)),
        dma((2, 4, 4)),
        dma((2, 4, 4)),
        dma((2, 4, 4)),
        dma((2, 8)),
        dma((2, 8)),
    ]
    shape = jax.ShapeDtypeStruct((16, 1024), F32)
    return pl.pallas_call(
        kernel,
        out_shape=(shape, shape),
        in_specs=[vmem] * 10 + [hbm] * 3,
        out_specs=(vmem, vmem),
        scratch_shapes=scratch,
        compiler_params=pltpu.CompilerParams(collective_id=0, has_side_effects=True, vmem_limit_bytes=50 << 20),
    )(states, gain.reshape(32, 128), ids, weights, ga, gb, ua, ub, da, db, gw, uw, dw)


def solution(mesh):
    return jax.shard_map(
        per_device,
        mesh=mesh,
        in_specs=(
            P(("replica", "expert"), "tensor"),
            P(),
            P(None, ("replica", "expert"), None),
            P(None, ("replica", "expert"), None),
            P("expert", None, "tensor"),
            P("expert", None, "tensor"),
            P("expert", "tensor", None),
            P("expert", "replica", None),
            P("expert", "replica", "tensor"),
            P("expert", "replica", None),
            P("expert", "replica", "tensor"),
            P("expert", "replica", "tensor"),
            P("expert", "replica", None),
        ),
        out_specs=(P(("replica", "expert"), "tensor"), P(("replica", "expert"), "tensor")),
        check_vma=False,
    )
```

```python
import jax
import jax.numpy as jnp
from jax import lax
from jax.experimental import pallas as pl
from jax.experimental.pallas import tpu as pltpu
from jax.sharding import PartitionSpec as P

EPS = 1e-06
MESH = pl.DeviceIdType.MESH
BF = jnp.bfloat16
F32 = jnp.float32
NT = (((1,), (1,)), ((), ()))
ORDER = (2, 1, 3, 0)


def kernel(
    states_in, gain_in, ids_in, weights_in, ga_in, gb_in, ua_in, ub_in, da_in, db_in, gw, uw, dw,
    out_state, out_update,
    states, gain, ids, weights, ga, gb, ua, ub, da, db,
    w, wd, abuf, sbuf, bd, adt, mixb, mixs, cur, upd, gs, gi, xb, acc, uacc, ssq, hbuf, vbuf, po, rb, s2, r2,
    isem, wsem, ad_s, ad_r, mx_s, mx_r, a1s, a1r, a2s, a2r, b1s, b1r, b2s, b2r,
):
    r, e, t = lax.axis_index("replica"), lax.axis_index("expert"), lax.axis_index("tensor")
    y, z = e // 2, e % 2
    core = r % 2
    half = r // 2
    far = r + 2 - 4 * half
    other = r + 1 - 2 * core
    across = r + core * (2 - 4 * half)

    ts = [t] + [(t + d) % 4 for d in range(1, 4)]
    ys = [y] + [(y + d) % 4 for d in range(1, 4)]
    zs = (z, 1 - z)

    def dev(dt=0, dy=0, dz=0):
        return (across if dz else r, ys[dy] * 2 + zs[dz], ts[dt])

    def peer(h, d, dz=0):
        return dev(dt=d, dz=dz) if h == 0 else dev(dy=d, dz=dz)

    def remote(src, dst, ss, rs, to):
        return pltpu.make_async_remote_copy(
            src_ref=src, dst_ref=dst, send_sem=ss, recv_sem=rs, device_id=to, device_id_type=MESH
        )

    plane = [(d, dz) for d in range(4) for dz in range(2) if (d, dz) != (0, 0)]
    everyone = [peer(0, d, dz) for d, dz in plane] + [peer(1, d, dz) for d, dz in plane if d]
    everyone += [(far, e, t), (other, e, t)]
    barrier = pltpu.get_barrier_semaphore()
    for to in everyone:
        pl.semaphore_signal(barrier, inc=1, device_id=to, device_id_type=MESH)

    def await_bytes(like, sem):
        pltpu.make_async_copy(like, like, sem).wait()

    small = (
        (states_in, states), (gain_in, gain), (ids_in, ids), (weights_in, weights), (ga_in, ga),
        (ua_in, ua), (gb_in, gb), (ub_in, ub), (da_in, da), (db_in, db),
    )
    small = [pltpu.make_async_copy(a, b, isem.at[i]) for i, (a, b) in enumerate(small)]
    for copy in small:
        copy.start()
    loads = []
    for j in range(2):
        for m, ref in enumerate((gw, uw)):
            loads.append((ref.at[j], w.at[:, pl.ds(j * 768 + m * 384, 384)]))
    for j in range(2):
        loads.append((dw.at[j], wd.at[pl.ds(j * 384, 384)]))
    loads = [pltpu.make_async_copy(a, b, wsem.at[i]) for i, (a, b) in enumerate(loads)]
    for copy in loads:
        copy.start()

    for copy in small:
        copy.wait()

    cur[...] = states[...].astype(F32)
    for c in range(8):
        row = jnp.concatenate([gain[pl.ds(4 * c + i, 1), :] for i in range(4)], axis=1)
        gs[c] = row
        gi[c] = 1.0 / row
    rows = lax.broadcasted_iota(jnp.int32, (128, 16), 0)
    mix = jnp.zeros((128, 16), F32)
    for s in range(3):
        raw = weights[s]
        raw = raw / jnp.sum(raw, axis=0, keepdims=True)
        chosen = ids[s]
        for k in range(4):
            mix = mix + jnp.where(rows == chosen[k : k + 1, :] + 16 * s, raw[k : k + 1, :], 0.0)
    mixb[y, z] = mix.T

    def pack(ref, scale):
        return (jnp.concatenate([ref[0].astype(F32), ref[1].astype(F32)], axis=0) * scale).astype(BF)

    abuf[r, 0] = pack(ga, 1.0)
    abuf[r, 1] = pack(ua, 1.0)
    sbuf[r, 0] = pack(gb, 2.0)
    sbuf[r, 1] = pack(ub, 2.0)
    sbuf[r, 2] = pack(da, 1.0)
    wd[pl.ds(pl.multiple_of(768 + 16 * r, 16), 16), :] = pack(db, 2.0)

    pl.semaphore_wait(barrier, len(everyone))

    def ranks(q, kind, to):
        rows = wd.at[pl.ds(pl.multiple_of(768 + 16 * q, 16), 16)]
        refs = (abuf.at[q], sbuf.at[q], rows)
        return [remote(x, x, ad_s.at[kind, i], ad_r.at[kind, i], to) for i, x in enumerate(refs)]

    to_far = ranks(r, 0, (far, e, t))
    to_other = ranks(r, 1, (other, e, t))
    passed_on = ranks(far, 2, (other, e, t))
    mixes = [
        remote(mixb.at[y, z], mixb.at[y, z], mx_s.at[2 * d + dz], mx_r.at[2 * d + dz], peer(1, d, dz)) for d, dz in plane
    ]

    def step(s, carry):
        for h in range(2):
            cols = slice(h * 512, h * 512 + 512)
            xb[h, t, y, z] = (cur[:, cols] * gs[2 * t + h]).astype(BF)
        for d, dz in ((2, 1), (1, 1), (3, 1), (2, 0), (0, 1), (1, 0), (3, 0)):
            for h in range(2):
                block = xb.at[h, t, y, z]
                remote(block, block, a1s.at[h], a1r.at[h, d], peer(h, d, dz)).start()

        def onward(h, d, block):
            for p in ORDER[:3]:
                group = d if h == 0 else p
                remote(block, block, a2s.at[h], a2r.at[h, group], peer(1 - h, p)).start()

        for h in range(2):
            onward(h, 0, xb.at[h, t, y, z])

        @pl.when(s == 0)
        def _():
            for copy in to_far + to_other + mixes:
                copy.start()

        for d in (0, 1, 3, 2):
            for h in range(2):
                await_bytes(s2.at[0, pl.ds(0, 2 if d else 1)], a1r.at[h, d])
                if d:
                    onward(h, d, xb.at[0, ts[4 - d], y] if h == 0 else xb.at[1, t, ys[4 - d]])
                else:
                    onward(h, 0, xb.at[h, t, y, zs[1]])

        @pl.when(s == 0)
        def _():
            for copy in loads:
                copy.wait()

        acc[...] = jnp.zeros_like(acc)
        ssq[...] = jnp.zeros_like(ssq)
        uacc[...] = jnp.zeros_like(uacc)

        def low_rank(h, tc, x):
            a = abuf[:, :, :, pl.ds(pl.multiple_of(tc * 1024 + h * 512, 512), 512)].reshape(128, 512)
            uacc[...] += lax.dot_general(x, a, NT, preferred_element_type=F32)

        def chunk(h, tc):
            x = xb[h, tc].reshape(128, 512)
            k0 = pl.multiple_of(tc * 1024 + h * 512, 512)
            for n in range(3):
                cols = slice(n * 512, n * 512 + 512)
                acc[:, cols] += jnp.dot(x, w[pl.ds(k0, 512), cols], preferred_element_type=F32)
            plain = x.astype(F32) * gi[2 * tc + h]
            plain = plain * plain
            ssq[...] += plain[:, :128] + plain[:, 128:256] + plain[:, 256:384] + plain[:, 384:]

            @pl.when(s > 0)
            def _():
                low_rank(h, tc, x)

        chunk(1, t)
        for d, p in ((0, 0), (1, 0), (3, 2), (2, 1)):
            await_bytes(rb.at[0, :, 0], a2r.at[0, d])
            chunk(0, ts[(4 - d) % 4])
            if p:
                await_bytes(po.at[0, 0], a2r.at[1, p])
                chunk(1, ts[4 - p])
            if d == 1:

                @pl.when(s == 0)
                def _():
                    to_far[0].wait_recv()
                    passed_on[0].start()

        await_bytes(po.at[0, 0], a2r.at[1, 3])
        chunk(1, ts[1])

        @pl.when(s == 0)
        def _():
            for i in (1, 2):
                to_far[i].wait_recv()
                passed_on[i].start()
            for copy in to_other + passed_on + mixes:
                copy.wait_recv()
            bd[...] = jnp.zeros_like(bd)
            for q in range(4):
                for j in range(2):
                    keep = lax.broadcasted_iota(jnp.int32, (16, 384), 0) // 8 == j
                    for m in range(2):
                        part = jnp.where(keep, sbuf[q, m].astype(F32), 0.0).astype(BF)
                        bd[q * 32 + m * 16 : q * 32 + m * 16 + 16, j * 768 + m * 384 : j * 768 + m * 384 + 384] = part
                    part = jnp.where(keep, sbuf[q, 2].astype(F32), 0.0).astype(BF)
                    adt[q * 16 : q * 16 + 16, j * 384 : j * 384 + 384] = part
            for tc in range(4):
                for h in range(2):
                    low_rank(h, tc, xb[h, tc].reshape(128, 512))
            for copy in to_far + to_other + passed_on + mixes:
                copy.wait_send()

        low = uacc[...].astype(BF)
        scale = lax.rsqrt(jnp.sum(ssq[...], axis=1, keepdims=True) * (1.0 / 4096.0) + EPS)
        mixed = mixb[...].reshape(128, 128)
        lanes = lax.broadcasted_iota(jnp.int32, (128, 128), 1)
        for j in range(2):
            here = jnp.sum(jnp.where(lanes == s * 16 + 2 * e + j, mixed, 0.0), axis=1, keepdims=True)
            for n in range(3):
                g0 = j * 768 + n * 128
                u0 = g0 + 384
                gate = acc[:, g0 : g0 + 128] + jnp.dot(low, bd[:, g0 : g0 + 128], preferred_element_type=F32)
                upper = acc[:, u0 : u0 + 128] + jnp.dot(low, bd[:, u0 : u0 + 128], preferred_element_type=F32)
                gate, upper = gate * scale, upper * scale
                hidden = gate / (1.0 + jnp.exp(-gate)) * upper * here
                hbuf[:, j * 384 + n * 128 : j * 384 + n * 128 + 128] = hidden.astype(BF)
        vbuf[...] = lax.dot_general(hbuf[...], adt[...], NT, preferred_element_type=F32).astype(BF)

        for d in ORDER:
            tc = ts[d]
            for h in (1, 0):
                k0 = pl.multiple_of(tc * 1024 + h * 512, 512)
                part = jnp.dot(hbuf[...], wd[0:768, pl.ds(k0, 512)], preferred_element_type=F32)
                part = part + jnp.dot(vbuf[...], wd[768:832, pl.ds(k0, 512)], preferred_element_type=F32)
                po[h, tc] = part.astype(BF).reshape(4, 2, 16, 512)
                if h == 0:
                    for p in ORDER[:3]:
                        remote(po.at[0, tc, ys[p]], rb.at[0, p - 1, tc], b1s.at[0], b1r.at[0, d], peer(1, p)).start()
                elif d:
                    for i in ORDER:
                        remote(po.at[1, tc, ys[i]], rb.at[1, d - 1, ys[i]], b1s.at[1], b1r.at[1, i], peer(0, d)).start()
        for h in range(2):
            await_bytes(s2.at[0, pl.ds(0, 7)], a1s.at[h])
            await_bytes(po.at[0, pl.ds(0, 3)], a2s.at[h])
        for d in ORDER:
            for h in range(2):
                await_bytes(rb.at[0, :, 0], b1r.at[h, d])
                i = ts[d] if h == 0 else ys[d]
                for dz in range(2):
                    zz = zs[dz]
                    own = po[0, i, y, zz] if h == 0 else po[1, t, i, zz]
                    total = own.astype(F32)
                    for p in range(3):
                        total = total + rb[h, p, i, zz].astype(F32)
                    if (d, dz) == (0, 0):
                        upd[:, h * 512 : h * 512 + 512] = total
                    else:
                        n = 2 * d + dz
                        s2[h, n] = total.astype(BF)
                        remote(s2.at[h, n], r2.at[h, n], b2s.at[h], b2r.at[h], peer(h, d, dz)).start()
        for h in range(2):
            await_bytes(po.at[0, pl.ds(0, 3)], b1s.at[h])
        for h in range(2):
            cols = slice(h * 512, h * 512 + 512)
            total = upd[:, cols]
            await_bytes(s2.at[0, pl.ds(0, 7)], b2r.at[h])
            for d, dz in plane:
                total = total + r2[h, 2 * d + dz].astype(F32)
            upd[:, cols] = total
            cur[:, cols] += total
        for h in range(2):
            await_bytes(s2.at[0, pl.ds(0, 7)], b2s.at[h])
        return carry

    lax.fori_loop(0, 3, step, 0)
    out_state[...] = cur[...]
    out_update[...] = upd[...]


def per_device(states, gain, ids, weights, gw, uw, dw, ga, gb, ua, ub, da, db):
    vmem = pl.BlockSpec(memory_space=pltpu.VMEM)
    hbm = pl.BlockSpec(memory_space=pltpu.HBM)
    dma = pltpu.SemaphoreType.DMA
    args = (states, gain.reshape(32, 128), jnp.swapaxes(ids, 1, 2), jnp.swapaxes(weights, 1, 2), ga, gb, ua, ub, da, db, gw, uw, dw)
    scratch = [pltpu.VMEM(x.shape, x.dtype) for x in args[:10]] + [
        pltpu.VMEM((4096, 1536), BF),
        pltpu.VMEM((832, 4096), BF),
        pltpu.VMEM((4, 2, 16, 4096), BF),
        pltpu.VMEM((4, 3, 16, 384), BF),
        pltpu.VMEM((128, 1536), BF),
        pltpu.VMEM((64, 768), BF),
        pltpu.VMEM((4, 2, 16, 128), F32),
        pltpu.VMEM((8, 128), F32),
        pltpu.VMEM((16, 1024), F32),
        pltpu.VMEM((16, 1024), F32),
        pltpu.VMEM((8, 1, 512), F32),
        pltpu.VMEM((8, 1, 512), F32),
        pltpu.VMEM((2, 4, 4, 2, 16, 512), BF),
        pltpu.VMEM((128, 1536), F32),
        pltpu.VMEM((128, 128), F32),
        pltpu.VMEM((128, 128), F32),
        pltpu.VMEM((128, 768), BF),
        pltpu.VMEM((128, 64), BF),
        pltpu.VMEM((2, 4, 4, 2, 16, 512), BF),
        pltpu.VMEM((2, 3, 4, 2, 16, 512), BF),
        pltpu.VMEM((2, 8, 16, 512), BF),
        pltpu.VMEM((2, 8, 16, 512), BF),
        dma((10,)),
        dma((6,)),
        dma((3, 3)),
        dma((3, 3)),
        dma((8,)),
        dma((8,)),
        dma((2,)),
        dma((2, 4)),
        dma((2,)),
        dma((2, 4)),
        dma((2,)),
        dma((2, 4)),
        dma((2,)),
        dma((2,)),
    ]
    shape = jax.ShapeDtypeStruct((16, 1024), F32)
    return pl.pallas_call(
        kernel,
        out_shape=(shape, shape),
        in_specs=[hbm] * 13,
        out_specs=(vmem, vmem),
        scratch_shapes=scratch,
        compiler_params=pltpu.CompilerParams(collective_id=0, has_side_effects=True, vmem_limit_bytes=62 << 20),
    )(*args)


def solution(mesh):
    return jax.shard_map(
        per_device,
        mesh=mesh,
        in_specs=(
            P(("replica", "expert"), "tensor"),
            P(),
            P(None, ("replica", "expert"), None),
            P(None, ("replica", "expert"), None),
            P("expert", None, "tensor"),
            P("expert", None, "tensor"),
            P("expert", "tensor", None),
            P("expert", "replica", None),
            P("expert", "replica", "tensor"),
            P("expert", "replica", None),
            P("expert", "replica", "tensor"),
            P("expert", "replica", "tensor"),
            P("expert", "replica", None),
        ),
        out_specs=(P(("replica", "expert"), "tensor"), P(("replica", "expert"), "tensor")),
        check_vma=False,
    )
```

```python
import jax
import jax.numpy as jnp
from jax import lax
from jax.experimental import pallas as pl
from jax.experimental.pallas import tpu as pltpu
from jax.sharding import PartitionSpec as P

EPS = 1e-06
MESH = pl.DeviceIdType.MESH
BF = jnp.bfloat16
F32 = jnp.float32
NT = (((1,), (1,)), ((), ()))
ORDER = (2, 1, 3, 0)


def kernel(
    states_in, gain_in, ids_in, weights_in, ga_in, gb_in, ua_in, ub_in, da_in, db_in, gw, uw, dw,
    out_state, out_update,
    states, gain, ids, weights, ga, gb, ua, ub, da, db,
    w, wd, abuf, sbuf, bd, adt, mixb, hs, cur, upd, gs, gi, xb, acc, uacc, ssq, hbuf, vbuf, po, rb, s2, r2,
    isem, wsem, ad_s, ad_r, mx_s, mx_r, a1s, a1r, a2s, a2r, b1s, b1r, b2s, b2r,
):
    r, e, t = lax.axis_index("replica"), lax.axis_index("expert"), lax.axis_index("tensor")
    y, z = e // 2, e % 2
    core = r % 2
    half = r // 2
    far = r + 2 - 4 * half
    other = r + 1 - 2 * core
    across = r + core * (2 - 4 * half)

    ts = [t] + [(t + d) % 4 for d in range(1, 4)]
    ys = [y] + [(y + d) % 4 for d in range(1, 4)]
    zs = (z, 1 - z)

    def dev(dt=0, dy=0, dz=0):
        return (across if dz else r, ys[dy] * 2 + zs[dz], ts[dt])

    def peer(h, d, dz=0):
        return dev(dt=d, dz=dz) if h == 0 else dev(dy=d, dz=dz)

    def remote(src, dst, ss, rs, to):
        return pltpu.make_async_remote_copy(
            src_ref=src, dst_ref=dst, send_sem=ss, recv_sem=rs, device_id=to, device_id_type=MESH
        )

    plane = [(d, dz) for d in range(4) for dz in range(2) if (d, dz) != (0, 0)]
    everyone = [peer(0, d, dz) for d, dz in plane] + [peer(1, d, dz) for d, dz in plane if d]
    everyone += [(far, e, t), (other, e, t)]
    barrier = pltpu.get_barrier_semaphore()
    for to in everyone:
        pl.semaphore_signal(barrier, inc=1, device_id=to, device_id_type=MESH)

    def await_bytes(like, sem):
        pltpu.make_async_copy(like, like, sem).wait()

    small = (
        (states_in, states), (gain_in, gain), (ids_in, ids), (weights_in, weights), (ga_in, ga),
        (ua_in, ua), (gb_in, gb), (ub_in, ub), (da_in, da), (db_in, db),
    )
    small = [pltpu.make_async_copy(a, b, isem.at[i]) for i, (a, b) in enumerate(small)]
    for copy in small:
        copy.start()
    loads = []
    for j in range(2):
        for m, ref in enumerate((gw, uw)):
            loads.append((ref.at[j], w.at[:, pl.ds(j * 768 + m * 384, 384)]))
    for j in range(2):
        loads.append((dw.at[j], wd.at[pl.ds(j * 384, 384)]))
    loads = [pltpu.make_async_copy(a, b, wsem.at[i]) for i, (a, b) in enumerate(loads)]
    for copy in loads:
        copy.start()

    for copy in small:
        copy.wait()

    cur[...] = states[...].astype(F32)
    for c in range(8):
        row = jnp.concatenate([gain[pl.ds(4 * c + i, 1), :] for i in range(4)], axis=1)
        gs[c] = row
        gi[c] = 1.0 / row
    rows = lax.broadcasted_iota(jnp.int32, (128, 16), 0)
    mix = jnp.zeros((128, 16), F32)
    for s in range(3):
        raw = weights[s]
        raw = raw / jnp.sum(raw, axis=0, keepdims=True)
        chosen = ids[s]
        for k in range(4):
            mix = mix + jnp.where(rows == chosen[k : k + 1, :] + 16 * s, raw[k : k + 1, :], 0.0)
    mixb[y, z] = mix.T

    def pack(ref, scale):
        return (jnp.concatenate([ref[0].astype(F32), ref[1].astype(F32)], axis=0) * scale).astype(BF)

    abuf[r, 0] = pack(ga, 1.0)
    abuf[r, 1] = pack(ua, 1.0)
    sbuf[r, 0] = pack(gb, 2.0)
    sbuf[r, 1] = pack(ub, 2.0)
    sbuf[r, 2] = pack(da, 1.0)
    wd[pl.ds(pl.multiple_of(768 + 16 * r, 16), 16), :] = pack(db, 2.0)

    pl.semaphore_wait(barrier, len(everyone))

    def ranks(q, kind, to):
        rows = wd.at[pl.ds(pl.multiple_of(768 + 16 * q, 16), 16)]
        refs = (abuf.at[q], sbuf.at[q], rows)
        return [remote(x, x, ad_s.at[kind, i], ad_r.at[kind, i], to) for i, x in enumerate(refs)]

    to_far = ranks(r, 0, (far, e, t))
    to_other = ranks(r, 1, (other, e, t))
    passed_on = ranks(far, 2, (other, e, t))
    mixes = [
        remote(mixb.at[y, z], mixb.at[y, z], mx_s.at[2 * d + dz], mx_r.at[2 * d + dz], peer(1, d, dz)) for d, dz in plane
    ]

    def step(s, carry):
        for h in range(2):
            cols = slice(h * 512, h * 512 + 512)
            xb[h, t, y, z] = (cur[:, cols] * gs[2 * t + h]).astype(BF)
        for d, dz in ((2, 1), (1, 1), (3, 1), (2, 0), (0, 1), (1, 0), (3, 0)):
            for h in range(2):
                block = xb.at[h, t, y, z]
                remote(block, block, a1s.at[h], a1r.at[h, d], peer(h, d, dz)).start()

        def onward(h, d, block):
            for p in ORDER[:3]:
                group = d if h == 0 else p
                remote(block, block, a2s.at[h], a2r.at[h, group], peer(1 - h, p)).start()

        for h in range(2):
            onward(h, 0, xb.at[h, t, y, z])

        @pl.when(s == 0)
        def _():
            for copy in mixes + to_far + to_other:
                copy.start()

        for d in (0, 1, 3, 2):
            for h in range(2):
                await_bytes(s2.at[0, pl.ds(0, 2 if d else 1)], a1r.at[h, d])
                if d:
                    onward(h, d, xb.at[0, ts[4 - d], y] if h == 0 else xb.at[1, t, ys[4 - d]])
                else:
                    onward(h, 0, xb.at[h, t, y, zs[1]])

        @pl.when(s == 0)
        def _():
            for copy in mixes:
                copy.wait_recv()

        mixed = mixb[...].reshape(128, 128)
        lanes = lax.broadcasted_iota(jnp.int32, (128, 128), 1)
        for j in range(2):
            here = jnp.sum(jnp.where(lanes == s * 16 + 2 * e + j, mixed, 0.0), axis=1, keepdims=True)
            hs[j] = jnp.broadcast_to(here, (128, 128))

        @pl.when(s == 0)
        def _():
            for copy in loads:
                copy.wait()

        acc[...] = jnp.zeros_like(acc)
        ssq[...] = jnp.zeros_like(ssq)
        uacc[...] = jnp.zeros_like(uacc)

        def low_rank(h, tc, x):
            a = abuf[:, :, :, pl.ds(pl.multiple_of(tc * 1024 + h * 512, 512), 512)].reshape(128, 512)
            uacc[...] += lax.dot_general(x, a, NT, preferred_element_type=F32)

        def chunk(h, tc):
            x = xb[h, tc].reshape(128, 512)
            k0 = pl.multiple_of(tc * 1024 + h * 512, 512)
            for n in range(3):
                cols = slice(n * 512, n * 512 + 512)
                acc[:, cols] += jnp.dot(x, w[pl.ds(k0, 512), cols], preferred_element_type=F32)
            plain = x.astype(F32) * gi[2 * tc + h]
            plain = plain * plain
            ssq[...] += plain[:, :128] + plain[:, 128:256] + plain[:, 256:384] + plain[:, 384:]

            @pl.when(s > 0)
            def _():
                low_rank(h, tc, x)

        chunk(1, t)
        for d, p in ((0, 0), (1, 0), (3, 2), (2, 1)):
            await_bytes(rb.at[0, :, 0], a2r.at[0, d])
            chunk(0, ts[(4 - d) % 4])
            if p:
                await_bytes(po.at[0, 0], a2r.at[1, p])
                chunk(1, ts[4 - p])
            if d == 1:

                @pl.when(s == 0)
                def _():
                    to_far[0].wait_recv()
                    passed_on[0].start()

        await_bytes(po.at[0, 0], a2r.at[1, 3])
        chunk(1, ts[1])

        @pl.when(s == 0)
        def _():
            to_far[1].wait_recv()
            passed_on[1].start()
            for copy in to_other[:2] + passed_on[:2]:
                copy.wait_recv()
            bd[...] = jnp.zeros_like(bd)
            for q in range(4):
                for j in range(2):
                    keep = lax.broadcasted_iota(jnp.int32, (16, 384), 0) // 8 == j
                    for m in range(2):
                        part = jnp.where(keep, sbuf[q, m].astype(F32), 0.0).astype(BF)
                        bd[q * 32 + m * 16 : q * 32 + m * 16 + 16, j * 768 + m * 384 : j * 768 + m * 384 + 384] = part
                    part = jnp.where(keep, sbuf[q, 2].astype(F32), 0.0).astype(BF)
                    adt[q * 16 : q * 16 + 16, j * 384 : j * 384 + 384] = part
            for tc in range(4):
                for h in range(2):
                    low_rank(h, tc, xb[h, tc].reshape(128, 512))
            to_far[2].wait_recv()
            passed_on[2].start()

        low = uacc[...].astype(BF)
        scale = lax.rsqrt(jnp.sum(ssq[...], axis=1, keepdims=True) * (1.0 / 4096.0) + EPS)
        for j in range(2):
            g0 = j * 768
            gates = acc[:, g0 : g0 + 384] + jnp.dot(low, bd[:, g0 : g0 + 384], preferred_element_type=F32)
            uppers = acc[:, g0 + 384 : g0 + 768] + jnp.dot(low, bd[:, g0 + 384 : g0 + 768], preferred_element_type=F32)
            weight = hs[j] * scale
            for n in range(3):
                half_gate = gates[:, n * 128 : n * 128 + 128] * (0.5 * scale)
                hidden = (half_gate + half_gate * jnp.tanh(half_gate)) * (uppers[:, n * 128 : n * 128 + 128] * weight)
                hbuf[:, j * 384 + n * 128 : j * 384 + n * 128 + 128] = hidden.astype(BF)
        vbuf[...] = lax.dot_general(hbuf[...], adt[...], NT, preferred_element_type=F32).astype(BF)

        @pl.when(s == 0)
        def _():
            for copy in (to_other[2], passed_on[2]):
                copy.wait_recv()
            for copy in to_far + to_other + passed_on + mixes:
                copy.wait_send()

        for d in ORDER:
            tc = ts[d]
            for h in (1, 0):
                k0 = pl.multiple_of(tc * 1024 + h * 512, 512)
                part = jnp.dot(hbuf[...], wd[0:768, pl.ds(k0, 512)], preferred_element_type=F32)
                part = part + jnp.dot(vbuf[...], wd[768:832, pl.ds(k0, 512)], preferred_element_type=F32)
                po[h, tc] = part.astype(BF).reshape(4, 2, 16, 512)
                if h == 0:
                    for p in ORDER[:3]:
                        remote(po.at[0, tc, ys[p]], rb.at[0, p - 1, tc], b1s.at[0], b1r.at[0, d], peer(1, p)).start()
                elif d:
                    for i in ORDER:
                        remote(po.at[1, tc, ys[i]], rb.at[1, d - 1, ys[i]], b1s.at[1], b1r.at[1, i], peer(0, d)).start()
        for h in range(2):
            await_bytes(s2.at[0, pl.ds(0, 7)], a1s.at[h])
            await_bytes(po.at[0, pl.ds(0, 3)], a2s.at[h])

        @pl.when(s > 0)
        def _():
            for h in range(2):
                await_bytes(s2.at[0, pl.ds(0, 7)], b2s.at[h])

        for d in ORDER:
            for h in range(2):
                await_bytes(rb.at[0, :, 0], b1r.at[h, d])
                i = ts[d] if h == 0 else ys[d]
                for dz in range(2):
                    zz = zs[dz]
                    own = po[0, i, y, zz] if h == 0 else po[1, t, i, zz]
                    total = own.astype(F32)
                    for p in range(3):
                        total = total + rb[h, p, i, zz].astype(F32)
                    if (d, dz) == (0, 0):
                        upd[:, h * 512 : h * 512 + 512] = total
                    else:
                        n = 2 * d + dz
                        s2[h, n] = total.astype(BF)
                        remote(s2.at[h, n], r2.at[h, n], b2s.at[h], b2r.at[h], peer(h, d, dz)).start()
        for h in range(2):
            await_bytes(po.at[0, pl.ds(0, 3)], b1s.at[h])
        for h in range(2):
            cols = slice(h * 512, h * 512 + 512)
            total = upd[:, cols]
            await_bytes(s2.at[0, pl.ds(0, 7)], b2r.at[h])
            for d, dz in plane:
                total = total + r2[h, 2 * d + dz].astype(F32)
            upd[:, cols] = total
            cur[:, cols] += total
        return carry

    lax.fori_loop(0, 3, step, 0)
    for h in range(2):
        await_bytes(s2.at[0, pl.ds(0, 7)], b2s.at[h])
    out_state[...] = cur[...]
    out_update[...] = upd[...]


def per_device(states, gain, ids, weights, gw, uw, dw, ga, gb, ua, ub, da, db):
    vmem = pl.BlockSpec(memory_space=pltpu.VMEM)
    hbm = pl.BlockSpec(memory_space=pltpu.HBM)
    dma = pltpu.SemaphoreType.DMA
    args = (states, gain.reshape(32, 128), jnp.swapaxes(ids, 1, 2), jnp.swapaxes(weights, 1, 2), ga, gb, ua, ub, da, db, gw, uw, dw)
    scratch = [pltpu.VMEM(x.shape, x.dtype) for x in args[:10]] + [
        pltpu.VMEM((4096, 1536), BF),
        pltpu.VMEM((832, 4096), BF),
        pltpu.VMEM((4, 2, 16, 4096), BF),
        pltpu.VMEM((4, 3, 16, 384), BF),
        pltpu.VMEM((128, 1536), BF),
        pltpu.VMEM((64, 768), BF),
        pltpu.VMEM((4, 2, 16, 128), F32),
        pltpu.VMEM((2, 128, 128), F32),
        pltpu.VMEM((16, 1024), F32),
        pltpu.VMEM((16, 1024), F32),
        pltpu.VMEM((8, 1, 512), F32),
        pltpu.VMEM((8, 1, 512), F32),
        pltpu.VMEM((2, 4, 4, 2, 16, 512), BF),
        pltpu.VMEM((128, 1536), F32),
        pltpu.VMEM((128, 128), F32),
        pltpu.VMEM((128, 128), F32),
        pltpu.VMEM((128, 768), BF),
        pltpu.VMEM((128, 64), BF),
        pltpu.VMEM((2, 4, 4, 2, 16, 512), BF),
        pltpu.VMEM((2, 3, 4, 2, 16, 512), BF),
        pltpu.VMEM((2, 8, 16, 512), BF),
        pltpu.VMEM((2, 8, 16, 512), BF),
        dma((10,)),
        dma((6,)),
        dma((3, 3)),
        dma((3, 3)),
        dma((8,)),
        dma((8,)),
        dma((2,)),
        dma((2, 4)),
        dma((2,)),
        dma((2, 4)),
        dma((2,)),
        dma((2, 4)),
        dma((2,)),
        dma((2,)),
    ]
    shape = jax.ShapeDtypeStruct((16, 1024), F32)
    return pl.pallas_call(
        kernel,
        out_shape=(shape, shape),
        in_specs=[hbm] * 13,
        out_specs=(vmem, vmem),
        scratch_shapes=scratch,
        compiler_params=pltpu.CompilerParams(collective_id=0, has_side_effects=True, vmem_limit_bytes=62 << 20),
    )(*args)


def solution(mesh):
    return jax.shard_map(
        per_device,
        mesh=mesh,
        in_specs=(
            P(("replica", "expert"), "tensor"),
            P(),
            P(None, ("replica", "expert"), None),
            P(None, ("replica", "expert"), None),
            P("expert", None, "tensor"),
            P("expert", None, "tensor"),
            P("expert", "tensor", None),
            P("expert", "replica", None),
            P("expert", "replica", "tensor"),
            P("expert", "replica", None),
            P("expert", "replica", "tensor"),
            P("expert", "replica", "tensor"),
            P("expert", "replica", None),
        ),
        out_specs=(P(("replica", "expert"), "tensor"), P(("replica", "expert"), "tensor")),
        check_vma=False,
    )
```

```python
import jax
import jax.numpy as jnp
from jax import lax
from jax.experimental import pallas as pl
from jax.experimental.pallas import tpu as pltpu
from jax.sharding import PartitionSpec as P

EPS = 1e-06
MESH = pl.DeviceIdType.MESH
BF = jnp.bfloat16
F32 = jnp.float32
NT = (((1,), (1,)), ((), ()))
ORDER = (2, 1, 3, 0)


def kernel(
    states_in, gain_in, ids_in, weights_in, ga_in, gb_in, ua_in, ub_in, da_in, db_in, gw, uw, dw,
    out,
    states, gain, ids, weights, ga, gb, ua, ub, da, db,
    w, wd, abuf, sbuf, bd, adt, mixb, hs, cur, upd, gs, gi, xb, acc, uacc, ssq, hbuf, vbuf, po, rb, s2, r2,
    isem, wsem, ad_s, ad_r, mx_s, mx_r, a1s, a1r, a2s, a2r, b1s, b1r, b2s, b2r,
):
    r, e, t = lax.axis_index("replica"), lax.axis_index("expert"), lax.axis_index("tensor")
    y, z = e // 2, e % 2
    core = r % 2
    half = r // 2
    far = r + 2 - 4 * half
    other = r + 1 - 2 * core
    across = r + core * (2 - 4 * half)

    ts = [t] + [(t + d) % 4 for d in range(1, 4)]
    ys = [y] + [(y + d) % 4 for d in range(1, 4)]
    zs = (z, 1 - z)

    def dev(dt=0, dy=0, dz=0):
        return (across if dz else r, ys[dy] * 2 + zs[dz], ts[dt])

    def peer(h, d, dz=0):
        return dev(dt=d, dz=dz) if h == 0 else dev(dy=d, dz=dz)

    def remote(src, dst, ss, rs, to):
        return pltpu.make_async_remote_copy(
            src_ref=src, dst_ref=dst, send_sem=ss, recv_sem=rs, device_id=to, device_id_type=MESH
        )

    plane = [(d, dz) for d in range(4) for dz in range(2) if (d, dz) != (0, 0)]
    everyone = [peer(0, d, dz) for d, dz in plane] + [peer(1, d, dz) for d, dz in plane if d]
    everyone += [(far, e, t), (other, e, t)]
    barrier = pltpu.get_barrier_semaphore()
    for to in everyone:
        pl.semaphore_signal(barrier, inc=1, device_id=to, device_id_type=MESH)

    def await_bytes(like, sem):
        pltpu.make_async_copy(like, like, sem).wait()

    small = (
        (states_in, states), (gain_in, gain), (ids_in, ids), (weights_in, weights), (ga_in, ga),
        (ua_in, ua), (gb_in, gb), (ub_in, ub), (da_in, da), (db_in, db),
    )
    small = [pltpu.make_async_copy(a, b, isem.at[i]) for i, (a, b) in enumerate(small)]
    for copy in small:
        copy.start()
    loads = []
    for j in range(2):
        for m, ref in enumerate((gw, uw)):
            loads.append((ref.at[j], w.at[:, pl.ds(j * 768 + m * 384, 384)]))
    for j in range(2):
        loads.append((dw.at[j], wd.at[pl.ds(j * 384, 384)]))
    loads = [pltpu.make_async_copy(a, b, wsem.at[i]) for i, (a, b) in enumerate(loads)]
    for copy in loads[:4]:
        copy.start()

    for copy in small:
        copy.wait()

    cur[...] = states[...].astype(F32)
    for c in range(8):
        row = jnp.concatenate([gain[pl.ds(4 * c + i, 1), :] for i in range(4)], axis=1)
        gs[c] = row
        gi[c] = 1.0 / row
    rows = lax.broadcasted_iota(jnp.int32, (128, 16), 0)
    mix = jnp.zeros((128, 16), F32)
    for s in range(3):
        raw = weights[s]
        raw = raw / jnp.sum(raw, axis=0, keepdims=True)
        chosen = ids[s]
        for k in range(4):
            mix = mix + jnp.where(rows == chosen[k : k + 1, :] + 16 * s, raw[k : k + 1, :], 0.0)
    mixb[y, z] = mix.T

    def pack(ref, scale):
        return (jnp.concatenate([ref[0].astype(F32), ref[1].astype(F32)], axis=0) * scale).astype(BF)

    abuf[r, 0] = pack(ga, 1.0)
    abuf[r, 1] = pack(ua, 1.0)
    sbuf[r, 0] = pack(gb, 2.0)
    sbuf[r, 1] = pack(ub, 2.0)
    sbuf[r, 2] = pack(da, 1.0)
    wd[pl.ds(pl.multiple_of(768 + 16 * r, 16), 16), :] = pack(db, 2.0)

    pl.semaphore_wait(barrier, len(everyone))

    def ranks(q, kind, to):
        rows = wd.at[pl.ds(pl.multiple_of(768 + 16 * q, 16), 16)]
        refs = (abuf.at[q], sbuf.at[q], rows)
        return [remote(x, x, ad_s.at[kind, i], ad_r.at[kind, i], to) for i, x in enumerate(refs)]

    to_far = ranks(r, 0, (far, e, t))
    to_other = ranks(r, 1, (other, e, t))
    passed_on = ranks(far, 2, (other, e, t))
    mixes = [
        remote(mixb.at[y, z], mixb.at[y, z], mx_s.at[2 * d + dz], mx_r.at[2 * d + dz], peer(1, d, dz)) for d, dz in plane
    ]

    def step(s, carry):
        for h in range(2):
            cols = slice(h * 512, h * 512 + 512)
            xb[h, t, y, z] = (cur[:, cols] * gs[2 * t + h]).astype(BF)
        for d, dz in ((2, 1), (1, 1), (3, 1), (2, 0), (0, 1), (1, 0), (3, 0)):
            for h in range(2):
                block = xb.at[h, t, y, z]
                remote(block, block, a1s.at[h], a1r.at[h, d], peer(h, d, dz)).start()

        def onward(h, d, block):
            for p in ORDER[:3]:
                group = d if h == 0 else p
                remote(block, block, a2s.at[h], a2r.at[h, group], peer(1 - h, p)).start()

        for h in range(2):
            onward(h, 0, xb.at[h, t, y, z])

        @pl.when(s == 0)
        def _():
            for copy in mixes + to_far + to_other:
                copy.start()

        for d in (0, 1, 3, 2):
            for h in range(2):
                await_bytes(s2.at[0, pl.ds(0, 2 if d else 1)], a1r.at[h, d])
                if d:
                    onward(h, d, xb.at[0, ts[4 - d], y] if h == 0 else xb.at[1, t, ys[4 - d]])
                else:
                    onward(h, 0, xb.at[h, t, y, zs[1]])

        @pl.when(s == 0)
        def _():
            for copy in mixes:
                copy.wait_recv()
            for copy in loads[4:]:
                copy.start()

        mixed = mixb[...].reshape(128, 128)
        lanes = lax.broadcasted_iota(jnp.int32, (128, 128), 1)
        for j in range(2):
            here = jnp.sum(jnp.where(lanes == s * 16 + 2 * e + j, mixed, 0.0), axis=1, keepdims=True)
            hs[j] = jnp.broadcast_to(here, (128, 128))

        @pl.when(s == 0)
        def _():
            for copy in loads:
                copy.wait()

        acc[...] = jnp.zeros_like(acc)
        ssq[...] = jnp.zeros_like(ssq)
        uacc[...] = jnp.zeros_like(uacc)

        def low_rank(h, tc, x):
            a = abuf[:, :, :, pl.ds(pl.multiple_of(tc * 1024 + h * 512, 512), 512)].reshape(128, 512)
            uacc[...] += lax.dot_general(x, a, NT, preferred_element_type=F32)

        def chunk(h, tc):
            x = xb[h, tc].reshape(128, 512)
            k0 = pl.multiple_of(tc * 1024 + h * 512, 512)
            for n in range(3):
                cols = slice(n * 512, n * 512 + 512)
                acc[:, cols] += jnp.dot(x, w[pl.ds(k0, 512), cols], preferred_element_type=F32)
            plain = x.astype(F32) * gi[2 * tc + h]
            plain = plain * plain
            ssq[...] += plain[:, :128] + plain[:, 128:256] + plain[:, 256:384] + plain[:, 384:]

            @pl.when(s > 0)
            def _():
                low_rank(h, tc, x)

        chunk(1, t)
        for d, p in ((0, 0), (1, 0), (3, 2), (2, 1)):
            await_bytes(rb.at[0, :, 0], a2r.at[0, d])
            chunk(0, ts[(4 - d) % 4])
            if p:
                await_bytes(po.at[0, 0], a2r.at[1, p])
                chunk(1, ts[4 - p])
            if d == 1:

                @pl.when(s == 0)
                def _():
                    to_far[0].wait_recv()
                    passed_on[0].start()

        await_bytes(po.at[0, 0], a2r.at[1, 3])
        chunk(1, ts[1])

        @pl.when(s == 0)
        def _():
            to_far[1].wait_recv()
            passed_on[1].start()
            for copy in to_other[:2] + passed_on[:2]:
                copy.wait_recv()
            bd[...] = jnp.zeros_like(bd)
            for q in range(4):
                for j in range(2):
                    keep = lax.broadcasted_iota(jnp.int32, (16, 384), 0) // 8 == j
                    for m in range(2):
                        part = jnp.where(keep, sbuf[q, m].astype(F32), 0.0).astype(BF)
                        bd[q * 32 + m * 16 : q * 32 + m * 16 + 16, j * 768 + m * 384 : j * 768 + m * 384 + 384] = part
                    part = jnp.where(keep, sbuf[q, 2].astype(F32), 0.0).astype(BF)
                    adt[q * 16 : q * 16 + 16, j * 384 : j * 384 + 384] = part
            for tc in range(4):
                for h in range(2):
                    low_rank(h, tc, xb[h, tc].reshape(128, 512))
            to_far[2].wait_recv()
            passed_on[2].start()

        low = uacc[...].astype(BF)
        scale = lax.rsqrt(jnp.sum(ssq[...], axis=1, keepdims=True) * (1.0 / 4096.0) + EPS)
        for j in range(2):
            g0 = j * 768
            gates = acc[:, g0 : g0 + 384] + jnp.dot(low, bd[:, g0 : g0 + 384], preferred_element_type=F32)
            uppers = acc[:, g0 + 384 : g0 + 768] + jnp.dot(low, bd[:, g0 + 384 : g0 + 768], preferred_element_type=F32)
            weight = hs[j] * scale
            for n in range(3):
                half_gate = gates[:, n * 128 : n * 128 + 128] * (0.5 * scale)
                hidden = (half_gate + half_gate * jnp.tanh(half_gate)) * (uppers[:, n * 128 : n * 128 + 128] * weight)
                hbuf[:, j * 384 + n * 128 : j * 384 + n * 128 + 128] = hidden.astype(BF)
        vbuf[...] = lax.dot_general(hbuf[...], adt[...], NT, preferred_element_type=F32).astype(BF)

        @pl.when(s == 0)
        def _():
            for copy in (to_other[2], passed_on[2]):
                copy.wait_recv()
            for copy in to_far + to_other + passed_on + mixes:
                copy.wait_send()

        for d in ORDER:
            tc = ts[d]
            for h in (1, 0):
                k0 = pl.multiple_of(tc * 1024 + h * 512, 512)
                part = jnp.dot(hbuf[...], wd[0:768, pl.ds(k0, 512)], preferred_element_type=F32)
                part = part + jnp.dot(vbuf[...], wd[768:832, pl.ds(k0, 512)], preferred_element_type=F32)
                po[h, tc] = part.astype(BF).reshape(4, 2, 16, 512)
                if h == 0:
                    for p in ORDER[:3]:
                        remote(po.at[0, tc, ys[p]], rb.at[0, p - 1, tc], b1s.at[0], b1r.at[0, d], peer(1, p)).start()
                elif d:
                    for i in ORDER:
                        remote(po.at[1, tc, ys[i]], rb.at[1, d - 1, ys[i]], b1s.at[1], b1r.at[1, i], peer(0, d)).start()
        for h in range(2):
            await_bytes(s2.at[0, pl.ds(0, 7)], a1s.at[h])
            await_bytes(po.at[0, pl.ds(0, 3)], a2s.at[h])

        @pl.when(s > 0)
        def _():
            for h in range(2):
                await_bytes(s2.at[0, pl.ds(0, 7)], b2s.at[h])

        for d in ORDER:
            for h in range(2):
                await_bytes(rb.at[0, :, 0], b1r.at[h, d])
                i = ts[d] if h == 0 else ys[d]
                for dz in range(2):
                    zz = zs[dz]
                    own = po[0, i, y, zz] if h == 0 else po[1, t, i, zz]
                    total = own.astype(F32)
                    for p in range(3):
                        total = total + rb[h, p, i, zz].astype(F32)
                    if (d, dz) == (0, 0):
                        upd[:, h * 512 : h * 512 + 512] = total
                    else:
                        n = 2 * d + dz
                        s2[h, n] = total.astype(BF)
                        remote(s2.at[h, n], r2.at[h, n], b2s.at[h], b2r.at[h], peer(h, d, dz)).start()
        for h in range(2):
            await_bytes(po.at[0, pl.ds(0, 3)], b1s.at[h])
        for h in range(2):
            cols = slice(h * 512, h * 512 + 512)
            total = upd[:, cols]
            await_bytes(s2.at[0, pl.ds(0, 7)], b2r.at[h])
            for d, dz in plane:
                total = total + r2[h, 2 * d + dz].astype(F32)
            upd[:, cols] = total
            cur[:, cols] += total
        return carry

    lax.fori_loop(0, 3, step, 0)
    for h in range(2):
        await_bytes(s2.at[0, pl.ds(0, 7)], b2s.at[h])
    out[0] = cur[...]
    out[1] = upd[...]


def per_device(states, gain, ids, weights, gw, uw, dw, ga, gb, ua, ub, da, db):
    vmem = pl.BlockSpec(memory_space=pltpu.VMEM)
    hbm = pl.BlockSpec(memory_space=pltpu.HBM)
    dma = pltpu.SemaphoreType.DMA
    args = (states, gain.reshape(32, 128), jnp.swapaxes(ids, 1, 2), jnp.swapaxes(weights, 1, 2), ga, gb, ua, ub, da, db, gw, uw, dw)
    scratch = [pltpu.VMEM(x.shape, x.dtype) for x in args[:10]] + [
        pltpu.VMEM((4096, 1536), BF),
        pltpu.VMEM((832, 4096), BF),
        pltpu.VMEM((4, 2, 16, 4096), BF),
        pltpu.VMEM((4, 3, 16, 384), BF),
        pltpu.VMEM((128, 1536), BF),
        pltpu.VMEM((64, 768), BF),
        pltpu.VMEM((4, 2, 16, 128), F32),
        pltpu.VMEM((2, 128, 128), F32),
        pltpu.VMEM((16, 1024), F32),
        pltpu.VMEM((16, 1024), F32),
        pltpu.VMEM((8, 1, 512), F32),
        pltpu.VMEM((8, 1, 512), F32),
        pltpu.VMEM((2, 4, 4, 2, 16, 512), BF),
        pltpu.VMEM((128, 1536), F32),
        pltpu.VMEM((128, 128), F32),
        pltpu.VMEM((128, 128), F32),
        pltpu.VMEM((128, 768), BF),
        pltpu.VMEM((128, 64), BF),
        pltpu.VMEM((2, 4, 4, 2, 16, 512), BF),
        pltpu.VMEM((2, 3, 4, 2, 16, 512), BF),
        pltpu.VMEM((2, 8, 16, 512), BF),
        pltpu.VMEM((2, 8, 16, 512), BF),
        dma((10,)),
        dma((6,)),
        dma((3, 3)),
        dma((3, 3)),
        dma((8,)),
        dma((8,)),
        dma((2,)),
        dma((2, 4)),
        dma((2,)),
        dma((2, 4)),
        dma((2,)),
        dma((2, 4)),
        dma((2,)),
        dma((2,)),
    ]
    both = pl.pallas_call(
        kernel,
        out_shape=jax.ShapeDtypeStruct((2, 16, 1024), F32),
        in_specs=[hbm] * 13,
        out_specs=vmem,
        scratch_shapes=scratch,
        compiler_params=pltpu.CompilerParams(collective_id=0, has_side_effects=True, vmem_limit_bytes=62 << 20),
    )(*args)
    return both[0], both[1]


def solution(mesh):
    return jax.shard_map(
        per_device,
        mesh=mesh,
        in_specs=(
            P(("replica", "expert"), "tensor"),
            P(),
            P(None, ("replica", "expert"), None),
            P(None, ("replica", "expert"), None),
            P("expert", None, "tensor"),
            P("expert", None, "tensor"),
            P("expert", "tensor", None),
            P("expert", "replica", None),
            P("expert", "replica", "tensor"),
            P("expert", "replica", None),
            P("expert", "replica", "tensor"),
            P("expert", "replica", "tensor"),
            P("expert", "replica", None),
        ),
        out_specs=(P(("replica", "expert"), "tensor"), P(("replica", "expert"), "tensor")),
        check_vma=False,
    )
```
